512 devices in a mesh: gx: 8 (over z_lo, x), gy: 8 (over y), gz: 8 (over z_hi, core).
Axes of the slice: x: 4, y: 8, z: 8 (z_hi: 4, z_lo: 2; z = z_hi * 2 + z_lo), core: 2. Of those that a mesh axis runs over, the one named last changes fastest.
Arguments:
- grad_act: bfloat16 [3072, 24576], P('gz', ('gy', 'gx')), may hold values from -6 to 6
- pre_act: bfloat16 [3072, 24576], P('gz', ('gy', 'gx')), may hold values from -8 to 8
- inputs: bfloat16 [3072, 6144], P('gz', 'gx'), may hold values from -0.109375 to 0.109375
- weight: bfloat16 [6144, 24576], P('gx', ('gy', 'gz')), may hold values from -0.21875 to 0.21875
Outputs:
- grad_inputs: bfloat16 [3072, 6144], P('gz', ('gx', 'gy'))
- grad_weight: bfloat16 [6144, 24576], P('gx', ('gy', 'gz'))
The draws below stay inside these ranges and needn't reach their ends.
All inputs are finite; a program needn't handle non-finite values.
Results may differ from the reference program's by a relative error of at most 0.0058.
Values may be sent and summed in bfloat16 or wider, within the bound.
A program may use at most 64 MiB of HBM per device.

```python
import jax
import jax.numpy as jnp
from jax import lax

D = 6144
FF = 24576
TOK_Z = 384
TOKENS = 3072
N_GZ = 8


def spiked(array, stream_key, source, target, parts, factor):
    def block_of(axis_at):
        return (jnp.arange(array.shape[axis_at]) // (array.shape[axis_at] // parts)).reshape((-1,) + (1,) * (array.ndim - 1 - axis_at))

    one_side = jax.random.permutation(stream_key, parts)[block_of(target)]
    second = (block_of(target) + parts // 2) % parts
    return jnp.where((block_of(source) == one_side) | (block_of(source) == second), factor * array, array)


def level_of(stream_key, dims, split, smallest, largest):
    def one(axis_at, blocks):
        draws = jax.random.uniform(jax.random.fold_in(jax.random.fold_in(stream_key, 6), axis_at), (blocks,), jnp.float32, smallest / len(split), largest / len(split))
        return jnp.repeat(jnp.exp(draws), dims[axis_at] // blocks).reshape((-1,) + (1,) * (len(dims) - axis_at - 1))

    level = one(*split[0])
    for cut in split[1:]:
        level = level * one(*cut)
    return level


def centred(key, dims, spread, reach, cuts=(), dtype=jnp.bfloat16):
    array = spread * jax.random.normal(key, dims, jnp.float32)
    if cuts:
        array = array * level_of(key, dims, cuts, -0.22, 0.18)
    return jnp.clip(array, -reach, reach).astype(dtype)


def bell_draw_with(key, shape, deviation, bound, cuts, heavy, held_as=jnp.bfloat16):
    result = deviation * jax.random.normal(key, shape, jnp.float32)
    if cuts:
        result = result * level_of(key, shape, cuts, -0.22, 0.18)
    return jnp.clip(spiked(result, jax.random.fold_in(key, 3), *heavy), -bound, bound).astype(held_as)


def setup_inputs(seed: int = 0) -> dict:
    splits = jax.random.split(jax.random.key(seed), 5)
    return {
        "grad_act": centred(splits[0], (TOKENS, FF), 1.0, 6.0, ((0, 8), (1, 64))),
        "pre_act": centred(splits[1], (TOKENS, FF), 1.5, 8.0, ((0, 8), (1, 64))),
        "inputs": centred(splits[2], (TOKENS, D), TOKENS ** -0.5, 0.109375, ((0, 8), (1, 8))),
        "weight": bell_draw_with(splits[3], (D, FF), D ** -0.5, 0.21875, ((0, 8), (1, 64)), (1, 0, 64, 4.0)),
    }


root_half = 0.7071067811865476
inv_root_tau = 0.3989422804014327

def gelu_grad(grad_act, pre_act):
    value = pre_act.astype(jnp.float32)
    cdf = 0.5 * (1.0 + jax.scipy.special.erf(value * root_half))
    pdf = jnp.exp(-0.5 * value * value) * inv_root_tau
    return (grad_act.astype(jnp.float32) * (cdf + value * pdf)).astype(jnp.bfloat16)

def reference(grad_act, pre_act, inputs, weight):
    grad_hidden = gelu_grad(grad_act, pre_act)
    grad_inputs = jnp.dot(grad_hidden, weight.T, preferred_element_type=jnp.float32).astype(jnp.bfloat16)
    hidden_blocks = grad_hidden.reshape(N_GZ, TOK_Z, FF)
    input_blocks = inputs.reshape(N_GZ, TOK_Z, D)

    def add_block(total, pair):
        rows_in, rows_hidden = pair
        part = jnp.dot(rows_in.T, rows_hidden, preferred_element_type=jnp.float32).astype(jnp.bfloat16)
        part = lax.optimization_barrier(part)
        return (total + part.astype(jnp.float32), None)
    total, unused = lax.scan(add_block, jnp.zeros((D, FF), jnp.float32), (input_blocks, hidden_blocks))
    return (grad_inputs, total.astype(jnp.bfloat16))
```

```python
import functools

import jax
import jax.numpy as jnp
from jax import lax
from jax.experimental import pallas as pl
from jax.experimental.pallas import tpu as pltpu
from jax.sharding import PartitionSpec as P

MESH = pl.DeviceIdType.MESH
root_half = 0.7071067811865476
inv_root_tau = 0.3989422804014327

TOK, FEAT, HID = 384, 768, 384
NY, NZ, NX = 8, 4, 4
SLICE = FEAT // NY
HALF = SLICE // 2
ORDER = (0, 1, 3, 2)


def gelu_grad(grad_act, pre_act):
    value = pre_act.astype(jnp.float32)
    cdf = 0.5 * (1.0 + lax.erf(value * root_half))
    pdf = jnp.exp(-0.5 * value * value) * inv_root_tau
    return (grad_act.astype(jnp.float32) * (cdf + value * pdf)).astype(jnp.bfloat16)


def mod(value, size):
    return lax.rem(value + size, size)


def kernel(
    ga, pa, inp, w, git, gw,
    gh, ghs, inputs_t, total, pair_out, pair_in, up_out, down_out, up_in, down_in, z_out, z_in, acc,
    send_sem, gh_sem, col_sem, ring_sem, core_sem, pair_sem, up_sem, down_sem, z_sem,
):
    gx, y, gz = (lax.axis_index(name) for name in ("gx", "gy", "gz"))
    zl, x = lax.div(gx, NX), lax.rem(gx, NX)
    zh, c = lax.div(gz, 2), lax.rem(gz, 2)

    def device(x=x, zl=zl, y=y, zh=zh, c=c):
        return (zl * NX + x, y, zh * 2 + c)

    other_core = device(c=1 - c)
    above, below = device(y=mod(y + 1, NY)), device(y=mod(y - 1, NY))
    at_z = [device(zh=mod(zh + k, NZ)) for k in range(NZ)]

    home_zh, home_c = lax.div(x, 2) + 2 * zl, lax.rem(x, 2)
    at_home = jnp.logical_and(home_zh == zh, home_c == c)
    root_x = 2 * lax.rem(zh, 2) + c
    step_x = 2 * c - 1
    role = lax.rem((x - root_x) * step_x + 2 * NX, NX)
    is_root, is_relay = role == 0, role == 1
    onward, backward = device(x=mod(x + step_x, NX)), device(x=mod(x - step_x, NX))

    barrier = pltpu.get_barrier_semaphore()

    def hello(dev):
        pl.semaphore_signal(barrier, inc=1, device_id=dev, device_id_type=MESH)

    for dev in (other_core, above, below, onward, backward, at_z[1], at_z[2], at_z[3]):
        hello(dev)
    src_zl = lax.div(zh, 2)
    for k in range(NZ):
        for core in range(2):
            here = jnp.logical_and(zl == src_zl, jnp.logical_and(zh == k, c == core))

            @pl.when(jnp.logical_and(is_root, jnp.logical_not(here)))
            def _():
                hello(device(zl=src_zl, zh=k, c=core))
    pl.semaphore_wait(barrier, 10 - at_home.astype(jnp.int32))

    sends = []

    def remote(src, dst, recv, dev, cond=None):
        copy = pltpu.make_async_remote_copy(
            src_ref=src, dst_ref=dst, send_sem=send_sem.at[len(sends)], recv_sem=recv,
            device_id=dev, device_id_type=MESH,
        )
        sends.append((copy, cond))
        if cond is None:
            copy.start()
        else:
            pl.when(cond)(copy.start)

    def arrived(dst, recv):
        pltpu.make_async_remote_copy(
            src_ref=dst, dst_ref=dst, send_sem=send_sem.at[0], recv_sem=recv,
            device_id=other_core, device_id_type=MESH,
        ).wait_recv()

    for r in range(0, TOK, 64):
        gh[r : r + 64, :] = gelu_grad(ga[r : r + 64, :], pa[r : r + 64, :])
    far = mod(zh - home_zh, NZ)
    for zl_to in range(2):
        local = jnp.logical_and(at_home, zl == zl_to)
        remote(
            gh, ghs.at[far, c], gh_sem.at[far * 2 + c],
            device(zl=zl_to, zh=home_zh, c=home_c), jnp.logical_not(local),
        )

        @pl.when(local)
        def _():
            pltpu.make_async_copy(gh, ghs.at[0, c], gh_sem.at[c]).start()

    inputs_t[c, 0] = inp[...].astype(jnp.float32).T.astype(jnp.bfloat16).reshape(NY, SLICE, TOK)
    for k in range(1, NZ):
        remote(inputs_t.at[c, 0, y], inputs_t.at[c, k, y], col_sem.at[k - 1], at_z[NZ - k])
    remote(inputs_t.at[c, 0], inputs_t.at[c, 0], core_sem.at[0], other_core)

    def piece(who, rows=None):
        who = mod(who, NY)
        if rows is None:
            return inputs_t.at[c, pl.ds(1, NZ - 1), who]
        return inputs_t.at[c, pl.ds(1, NZ - 1), who, pl.ds(rows, HALF)]

    def inputs_ring(step):
        if step == 0:
            for k in range(1, NZ):
                arrived(inputs_t.at[c, k, y], col_sem.at[k - 1])
        elif step < 4:
            arrived(piece(y - step), ring_sem.at[step - 1])
            arrived(piece(y + step), ring_sem.at[4 + step - 1])
        else:
            arrived(piece(y - 4, 0), ring_sem.at[3])
            arrived(piece(y + 4, HALF), ring_sem.at[7])
            rest = inputs_t.at[c, pl.ds(1, NZ - 1)]
            remote(rest, rest, core_sem.at[1], other_core)
            return
        lo, hi = (0, HALF) if step == 3 else (None, None)
        remote(piece(y - step, lo), piece(y - step, lo), ring_sem.at[step], above)
        remote(piece(y + step, hi), piece(y + step, hi), ring_sem.at[4 + step], below)

    def gather(k):
        for core in range(2):
            block, sem = ghs.at[k, core], gh_sem.at[2 * k + core]
            arrived(block, sem)
            remote(block, block, sem, onward, jnp.logical_or(is_root, is_relay))
            remote(block, block, sem, backward, is_root)

    def product(k, core):
        return lax.dot_general(
            w[...], ghs[k, core], (((1,), (1,)), ((), ())), preferred_element_type=jnp.float32
        ).reshape(NY, SLICE, TOK)

    def compute(k):
        pair_out[k] = product(k, 1 - c).astype(jnp.bfloat16)
        remote(pair_out.at[k], pair_in.at[k], pair_sem.at[k], other_core)
        total[k] = product(k, c)

    def add_pair(k):
        arrived(pair_in.at[k], pair_sem.at[k])
        total[k] = total[k] + pair_in[k].astype(jnp.float32)

    def reduce(k, step):
        up_to, down_to = mod(y + 5 - step, NY), mod(y - 5 + step, NY)
        up_dst, down_dst = up_in.at[k, step - 1], down_in.at[k, step - 1]
        up_src, down_src = up_out.at[k, step - 1], down_out.at[k, step - 1]
        lo, hi = pl.ds(0, HALF), pl.ds(HALF, HALF)
        if step == 1:
            up_out[k, 0, lo] = total[k, up_to, lo].astype(jnp.bfloat16)
            down_out[k, 0, hi] = total[k, down_to, hi].astype(jnp.bfloat16)
            up_src, up_dst = up_src.at[lo], up_dst.at[lo]
            down_src, down_dst = down_src.at[hi], down_dst.at[hi]
        elif step == 2:
            arrived(up_in.at[k, 0, lo], up_sem.at[4 * k])
            up_out[k, 1, lo] = (total[k, up_to, lo] + up_in[k, 0, lo].astype(jnp.float32)).astype(jnp.bfloat16)
            up_out[k, 1, hi] = total[k, up_to, hi].astype(jnp.bfloat16)
            arrived(down_in.at[k, 0, hi], down_sem.at[4 * k])
            down_out[k, 1, hi] = (total[k, down_to, hi] + down_in[k, 0, hi].astype(jnp.float32)).astype(jnp.bfloat16)
            down_out[k, 1, lo] = total[k, down_to, lo].astype(jnp.bfloat16)
        else:
            arrived(up_in.at[k, step - 2], up_sem.at[4 * k + step - 2])
            up_out[k, step - 1] = (total[k, up_to] + up_in[k, step - 2].astype(jnp.float32)).astype(jnp.bfloat16)
            arrived(down_in.at[k, step - 2], down_sem.at[4 * k + step - 2])
            down_out[k, step - 1] = (total[k, down_to] + down_in[k, step - 2].astype(jnp.float32)).astype(jnp.bfloat16)
        remote(up_src, up_dst, up_sem.at[4 * k + step - 1], above)
        remote(down_src, down_dst, down_sem.at[4 * k + step - 1], below)

    def finish(k):
        arrived(up_in.at[k, 3], up_sem.at[4 * k + 3])
        arrived(down_in.at[k, 3], down_sem.at[4 * k + 3])
        whole = total[k, y] + up_in[k, 3].astype(jnp.float32) + down_in[k, 3].astype(jnp.float32)
        if k == 0:
            total[0, y] = whole
        else:
            z_out[k - 1] = whole.astype(jnp.bfloat16)
            remote(z_out.at[k - 1], z_in.at[k - 1], z_sem.at[k - 1], at_z[k])

    def weight_grad(k):
        for core in range(2):
            term = lax.dot_general(
                inputs_t[core, k].reshape(FEAT, TOK), ghs[k, core], (((1,), (0,)), ((), ())),
                preferred_element_type=jnp.float32,
            )
            if k == 0 and core == 0:
                acc[...] = term
            else:
                acc[...] += term

    a, b, d, e = ORDER
    gather(a)
    inputs_ring(0)
    compute(a)
    add_pair(a)
    reduce(a, 1)
    inputs_ring(1)
    gather(b)
    compute(b)
    reduce(a, 2)
    add_pair(b)
    reduce(b, 1)
    reduce(a, 3)
    inputs_ring(2)
    gather(d)
    reduce(a, 4)
    reduce(b, 2)
    compute(d)
    add_pair(d)
    reduce(d, 1)
    finish(a)
    reduce(b, 3)
    inputs_ring(3)
    gather(e)
    reduce(b, 4)
    reduce(d, 2)
    compute(e)
    add_pair(e)
    reduce(e, 1)
    finish(b)
    reduce(d, 3)
    inputs_ring(4)
    reduce(e, 2)
    reduce(d, 4)
    arrived(inputs_t.at[1 - c, 0], core_sem.at[0])
    weight_grad(0)
    reduce(e, 3)
    finish(d)
    arrived(inputs_t.at[1 - c, pl.ds(1, NZ - 1)], core_sem.at[1])
    weight_grad(1)
    reduce(e, 4)
    weight_grad(2)
    weight_grad(3)
    gw[...] = acc[...].astype(jnp.bfloat16)
    finish(e)
    for k in range(NZ - 1):
        arrived(z_in.at[k], z_sem.at[k])
    out = total[0, y]
    for k in range(NZ - 1):
        out = out + z_in[k].astype(jnp.float32)
    git[...] = out.astype(jnp.bfloat16)

    for copy, cond in sends:
        if cond is None:
            copy.wait_send()
        else:
            pl.when(cond)(copy.wait_send)


N_SENDS = 2 + 4 + 8 + 1 + 16 + 4 + 32 + 3


def shards(grad_act, pre_act, inputs, weight):
    vmem = pl.BlockSpec(memory_space=pltpu.VMEM)
    bf16, f32 = jnp.bfloat16, jnp.float32
    dma = pltpu.SemaphoreType.DMA
    git, gw = pl.pallas_call(
        kernel,
        out_shape=(
            jax.ShapeDtypeStruct((SLICE, TOK), bf16),
            jax.ShapeDtypeStruct((FEAT, HID), bf16),
        ),
        in_specs=[vmem] * 4,
        out_specs=(vmem, vmem),
        scratch_shapes=[
            pltpu.VMEM((TOK, HID), bf16),
            pltpu.VMEM((NZ, 2, TOK, HID), bf16),
            pltpu.VMEM((2, NZ, NY, SLICE, TOK), bf16),
            pltpu.VMEM((NZ, NY, SLICE, TOK), f32),
            pltpu.VMEM((NZ, NY, SLICE, TOK), bf16),
            pltpu.VMEM((NZ, NY, SLICE, TOK), bf16),
            pltpu.VMEM((NZ, 4, SLICE, TOK), bf16),
            pltpu.VMEM((NZ, 4, SLICE, TOK), bf16),
            pltpu.VMEM((NZ, 4, SLICE, TOK), bf16),
            pltpu.VMEM((NZ, 4, SLICE, TOK), bf16),
            pltpu.VMEM((NZ - 1, SLICE, TOK), bf16),
            pltpu.VMEM((NZ - 1, SLICE, TOK), bf16),
            pltpu.VMEM((FEAT, HID), f32),
            dma((N_SENDS,)),
            dma((2 * NZ,)),
            dma((NZ - 1,)),
            dma((8,)),
            dma((2,)),
            dma((NZ,)),
            dma((4 * NZ,)),
            dma((4 * NZ,)),
            dma((NZ - 1,)),
        ],
        compiler_params=pltpu.CompilerParams(
            collective_id=0, has_side_effects=True, vmem_limit_bytes=48 * 2**20
        ),
    )(grad_act, pre_act, inputs, weight)
    return git.T, gw


def solution(mesh):
    return jax.shard_map(
        shards,
        mesh=mesh,
        in_specs=(
            P("gz", ("gy", "gx")),
            P("gz", ("gy", "gx")),
            P("gz", "gx"),
            P("gx", ("gy", "gz")),
        ),
        out_specs=(P("gz", ("gx", "gy")), P("gx", ("gy", "gz"))),
        check_vma=False,
    )
```

```python
import functools

import jax
import jax.numpy as jnp
from jax import lax
from jax.experimental import pallas as pl
from jax.experimental.pallas import tpu as pltpu
from jax.sharding import PartitionSpec as P

MESH = pl.DeviceIdType.MESH
root_half = 0.7071067811865476
inv_root_tau = 0.3989422804014327

TOK, FEAT, HID = 384, 768, 384
NY, NZ, NX = 8, 4, 4
SLICE = FEAT // NY
HALF = SLICE // 2
PARTS = 2
ROWS = TOK // PARTS
ONE_ROW = (1,)


def gelu_grad(grad_act, pre_act):
    value = pre_act.astype(jnp.float32)
    cdf = 0.5 * (1.0 + lax.erf(value * root_half))
    pdf = jnp.exp(-0.5 * value * value) * inv_root_tau
    return (grad_act.astype(jnp.float32) * (cdf + value * pdf)).astype(jnp.bfloat16)


def mod(value, size):
    return lax.rem(value + size, size)


def kernel(
    ga_any, pa_any, inp_any, w_any, git, gw,
    ga, pa, inp, w, gh, ghs, inputs_t, total, pair_out, pair_in, up_out, down_out, up_in, down_in, z_out, z_in, acc,
    load_sem, send_sem, gh_sem, col_sem, ring_sem, core_sem, pair_sem, up_sem, down_sem, z_sem,
):
    loads = [
        pltpu.make_async_copy(src, dst, load_sem.at[i])
        for i, (src, dst) in enumerate(((pa_any, pa), (ga_any, ga), (inp_any, inp), (w_any, w)))
    ]
    for copy in loads:
        copy.start()

    gx, y, gz = (lax.axis_index(name) for name in ("gx", "gy", "gz"))
    zl, x = lax.div(gx, NX), lax.rem(gx, NX)
    zh, c = lax.div(gz, 2), lax.rem(gz, 2)

    def device(x=x, zl=zl, y=y, zh=zh, c=c):
        return (zl * NX + x, y, zh * 2 + c)

    other_core = device(c=1 - c)
    above, below = device(y=mod(y + 1, NY)), device(y=mod(y - 1, NY))
    at_z = [device(zh=mod(zh + k, NZ)) for k in range(NZ)]

    home_zh, home_c = lax.div(x, 2) + 2 * zl, lax.rem(x, 2)
    at_home = jnp.logical_and(home_zh == zh, home_c == c)
    root_x = 2 * lax.rem(zh, 2) + c
    step_x = 2 * c - 1
    role = lax.rem((x - root_x) * step_x + 2 * NX, NX)
    is_root, is_relay = role == 0, role == 1
    onward, backward = device(x=mod(x + step_x, NX)), device(x=mod(x - step_x, NX))

    barrier = pltpu.get_barrier_semaphore()

    def hello(dev):
        pl.semaphore_signal(barrier, inc=1, device_id=dev, device_id_type=MESH)

    other_zl = device(zl=1 - zl)
    for dev in (other_core, above, below, onward, backward, other_zl, at_z[1], at_z[2], at_z[3]):
        hello(dev)

    def first_zl(k, owner_zl):
        return (owner_zl, 1, 1 - owner_zl, 0)[k]

    src_zl = lax.div(zh, 2)
    for k in range(NZ):
        for core in range(2):
            expected = jnp.logical_and(is_root, first_zl(k, src_zl) == zl)
            if k == 0:
                expected = jnp.logical_and(expected, c != core)

            @pl.when(expected)
            def _():
                hello(device(zl=src_zl, zh=mod(zh + k, NZ), c=core))

    sends = []

    def remote(src, dst, recv, dev, cond=None):
        copy = pltpu.make_async_remote_copy(
            src_ref=src, dst_ref=dst, send_sem=send_sem.at[len(sends)], recv_sem=recv,
            device_id=dev, device_id_type=MESH,
        )
        sends.append((copy, cond))
        if cond is None:
            copy.start()
        else:
            pl.when(cond)(copy.start)

    def arrived(dst, recv):
        pltpu.make_async_remote_copy(
            src_ref=dst, dst_ref=dst, send_sem=send_sem.at[0], recv_sem=recv,
            device_id=other_core, device_id_type=MESH,
        ).wait_recv()

    loads[0].wait()
    loads[1].wait()
    for r in range(0, TOK, 64):
        gh[r : r + 64, :] = gelu_grad(ga[r : r + 64, :], pa[r : r + 64, :])
    loads[2].wait()
    inputs_t[c, 0] = inp[...].astype(jnp.float32).T.astype(jnp.bfloat16).reshape(NY, SLICE, TOK)
    pl.semaphore_wait(barrier, 10 - at_home.astype(jnp.int32))

    def send_inputs():
        for k in range(1, NZ):
            remote(inputs_t.at[c, 0, y], inputs_t.at[c, k, y], col_sem.at[k - 1], at_z[NZ - k])

    far = mod(zh - home_zh, NZ)

    def hidden_part(k, core, part):
        return ghs.at[k, core, pl.ds(part * ROWS, ROWS)], gh_sem.at[(2 * k + core) * PARTS + part]

    def send_hidden(turn):
        first = jnp.where(far == 0, zl, jnp.where(far == 1, 1, jnp.where(far == 2, 1 - zl, 0)))
        for part in range(PARTS):
            block, sem = hidden_part(far, c, part)
            remote(
                gh.at[pl.ds(part * ROWS, ROWS)], block, sem,
                device(zl=first, zh=home_zh, c=home_c), jnp.logical_and(turn, jnp.logical_not(at_home)),
            )

    def keep_hidden():
        @pl.when(at_home)
        def _():
            for part in range(PARTS):
                block, sem = hidden_part(0, c, part)
                pltpu.make_async_copy(gh.at[pl.ds(part * ROWS, ROWS)], block, sem).start()

    def share_inputs():
        remote(inputs_t.at[c, 0], inputs_t.at[c, 0], core_sem.at[0], other_core)

    def piece(k, who, rows=None):
        block = inputs_t.at[c, k, mod(who, NY)]
        return block if rows is None else block.at[pl.ds(rows, HALF)]

    def inputs_ring(step):
        for k in range(1, NZ):
            up, down = 8 * (k - 1), 8 * (k - 1) + 4
            if step == 0:
                arrived(piece(k, y), col_sem.at[k - 1])
            elif step < 4:
                arrived(piece(k, y - step), ring_sem.at[up + step - 1])
                arrived(piece(k, y + step), ring_sem.at[down + step - 1])
            else:
                arrived(piece(k, y - 4, 0), ring_sem.at[up + 3])
                arrived(piece(k, y + 4, HALF), ring_sem.at[down + 3])
                remote(inputs_t.at[c, k], inputs_t.at[c, k], core_sem.at[k], other_core)
                continue
            lo, hi = (0, HALF) if step == 3 else (None, None)
            remote(piece(k, y - step, lo), piece(k, y - step, lo), ring_sem.at[up + step], above)
            remote(piece(k, y + step, hi), piece(k, y + step, hi), ring_sem.at[down + step], below)

    home_row = zl == src_zl
    near = 3 - 2 * zl
    groups = [jnp.where(home_row, *pair) for pair in ((0, near), (near, 0), (4 - near, 2), (2, 4 - near))]
    first_here = (True, home_row, jnp.logical_not(home_row), False)

    def both(*conds):
        return functools.reduce(jnp.logical_and, conds)

    def gather(n, who):
        k, first = groups[n], first_here[n]
        for part in range(PARTS):
            for core in range(2):
                block, sem = hidden_part(k, core, part)
                one_row = core in ONE_ROW

                @pl.when(who)
                def _():
                    arrived(block, sem)

                go = who
                if one_row:
                    go = None if first is False else both(who, first)
                if go is not None and (who is is_root or who is is_relay):
                    remote(block, block, sem, onward, go)
                if go is not None and who is is_root:
                    remote(block, block, sem, backward, go)
                if first is not False and (who is is_root or one_row):
                    remote(block, block, sem, other_zl, both(who, first))

    is_leaf = role >= 2

    def product(k, core):
        return lax.dot_general(
            w[...], ghs[k, core], (((1,), (1,)), ((), ())), preferred_element_type=jnp.float32
        ).reshape(NY, SLICE, TOK)

    def compute(n):
        k = groups[n]
        pair_out[k] = product(k, 1 - c).astype(jnp.bfloat16)
        remote(pair_out.at[k], pair_in.at[k], pair_sem.at[k], other_core)
        total[k] = product(k, c)

    def add_pair(n):
        k = groups[n]
        arrived(pair_in.at[k], pair_sem.at[k])
        total[k] = total[k] + pair_in[k].astype(jnp.float32)

    def reduce(n, step):
        k = groups[n]
        up_to, down_to = mod(y + 5 - step, NY), mod(y - 5 + step, NY)
        up_dst, down_dst = up_in.at[k, step - 1], down_in.at[k, step - 1]
        up_src, down_src = up_out.at[k, step - 1], down_out.at[k, step - 1]
        lo, hi = pl.ds(0, HALF), pl.ds(HALF, HALF)
        if step == 1:
            up_out[k, 0, lo] = total[k, up_to, lo].astype(jnp.bfloat16)
            down_out[k, 0, hi] = total[k, down_to, hi].astype(jnp.bfloat16)
            up_src, up_dst = up_src.at[lo], up_dst.at[lo]
            down_src, down_dst = down_src.at[hi], down_dst.at[hi]
        elif step == 2:
            arrived(up_in.at[k, 0, lo], up_sem.at[4 * k])
            up_out[k, 1, lo] = (total[k, up_to, lo] + up_in[k, 0, lo].astype(jnp.float32)).astype(jnp.bfloat16)
            up_out[k, 1, hi] = total[k, up_to, hi].astype(jnp.bfloat16)
            arrived(down_in.at[k, 0, hi], down_sem.at[4 * k])
            down_out[k, 1, hi] = (total[k, down_to, hi] + down_in[k, 0, hi].astype(jnp.float32)).astype(jnp.bfloat16)
            down_out[k, 1, lo] = total[k, down_to, lo].astype(jnp.bfloat16)
        else:
            arrived(up_in.at[k, step - 2], up_sem.at[4 * k + step - 2])
            up_out[k, step - 1] = (total[k, up_to] + up_in[k, step - 2].astype(jnp.float32)).astype(jnp.bfloat16)
            arrived(down_in.at[k, step - 2], down_sem.at[4 * k + step - 2])
            down_out[k, step - 1] = (total[k, down_to] + down_in[k, step - 2].astype(jnp.float32)).astype(jnp.bfloat16)
        remote(up_src, up_dst, up_sem.at[4 * k + step - 1], above)
        remote(down_src, down_dst, down_sem.at[4 * k + step - 1], below)

    def finish(n):
        k = groups[n]
        arrived(up_in.at[k, 3], up_sem.at[4 * k + 3])
        arrived(down_in.at[k, 3], down_sem.at[4 * k + 3])
        whole = total[k, y] + up_in[k, 3].astype(jnp.float32) + down_in[k, 3].astype(jnp.float32)
        total[k, y] = whole
        z_out[k] = whole.astype(jnp.bfloat16)
        remote(z_out.at[k], z_in.at[k], z_sem.at[k], device(zh=mod(zh + k, NZ)), k != 0)

    def weight_grad(k):
        arrived(inputs_t.at[1 - c, k], core_sem.at[k])
        for core in range(2):
            term = lax.dot_general(
                inputs_t[core, k].reshape(FEAT, TOK), ghs[k, core], (((1,), (0,)), ((), ())),
                preferred_element_type=jnp.float32,
            )
            if k == 0 and core == 0:
                acc[...] = term
            else:
                acc[...] += term

    def write_weight_grad():
        gw[...] = acc[...].astype(jnp.bfloat16)

    def write_inputs_grad():
        out = total[0, y]
        for k in range(1, NZ):
            arrived(z_in.at[k], z_sem.at[k])
            out = out + z_in[k].astype(jnp.float32)
        git[...] = out.astype(jnp.bfloat16)

    loads[3].wait()
    root, relay, leaf, role2, role3 = is_root, is_relay, is_leaf, role == 2, role == 3
    schedule = (
        (send_inputs,), (keep_hidden,), (send_hidden, far != 2), (share_inputs,), (gather, 0, root),
        (inputs_ring, 0), (gather, 1, root), (send_hidden, both(far == 2, root)), (gather, 0, role3), (send_hidden, both(far == 2, role3)),
        (gather, 0, relay), (inputs_ring, 1), (gather, 0, role2),
        (compute, 0), (gather, 2, root), (gather, 1, relay), (add_pair, 0), (reduce, 0, 1), (inputs_ring, 2),
        (gather, 3, root), (gather, 1, leaf), (compute, 1), (gather, 2, relay), (reduce, 0, 2), (inputs_ring, 3),
        (add_pair, 1), (reduce, 1, 1), (reduce, 0, 3), (gather, 2, leaf), (compute, 2), (inputs_ring, 4),
        (gather, 3, relay), (reduce, 1, 2), (reduce, 0, 4), (add_pair, 2), (reduce, 2, 1), (reduce, 1, 3),
        (finish, 0), (gather, 3, leaf), (compute, 3), (reduce, 2, 2), (reduce, 1, 4), (add_pair, 3), (reduce, 3, 1),
        (reduce, 2, 3), (finish, 1), (weight_grad, 0), (reduce, 3, 2), (reduce, 2, 4), (weight_grad, 1),
        (reduce, 3, 3), (finish, 2), (weight_grad, 2), (reduce, 3, 4), (weight_grad, 3), (write_weight_grad,),
        (finish, 3), (write_inputs_grad,),
    )
    for step, *args in schedule:
        step(*args)

    for copy, cond in sends:
        if cond is None:
            copy.wait_send()
        else:
            pl.when(cond)(copy.wait_send)


N_SENDS = 192


def shards(grad_act, pre_act, inputs, weight):
    vmem = pl.BlockSpec(memory_space=pltpu.VMEM)
    bf16, f32 = jnp.bfloat16, jnp.float32
    dma = pltpu.SemaphoreType.DMA
    git, gw = pl.pallas_call(
        kernel,
        out_shape=(
            jax.ShapeDtypeStruct((SLICE, TOK), bf16),
            jax.ShapeDtypeStruct((FEAT, HID), bf16),
        ),
        in_specs=[pl.BlockSpec(memory_space=pl.ANY)] * 4,
        out_specs=(vmem, vmem),
        scratch_shapes=[
            pltpu.VMEM((TOK, HID), bf16),
            pltpu.VMEM((TOK, HID), bf16),
            pltpu.VMEM((TOK, FEAT), bf16),
            pltpu.VMEM((FEAT, HID), bf16),
            pltpu.VMEM((TOK, HID), bf16),
            pltpu.VMEM((NZ, 2, TOK, HID), bf16),
            pltpu.VMEM((2, NZ, NY, SLICE, TOK), bf16),
            pltpu.VMEM((NZ, NY, SLICE, TOK), f32),
            pltpu.VMEM((NZ, NY, SLICE, TOK), bf16),
            pltpu.VMEM((NZ, NY, SLICE, TOK), bf16),
            pltpu.VMEM((NZ, 4, SLICE, TOK), bf16),
            pltpu.VMEM((NZ, 4, SLICE, TOK), bf16),
            pltpu.VMEM((NZ, 4, SLICE, TOK), bf16),
            pltpu.VMEM((NZ, 4, SLICE, TOK), bf16),
            pltpu.VMEM((NZ, SLICE, TOK), bf16),
            pltpu.VMEM((NZ, SLICE, TOK), bf16),
            pltpu.VMEM((FEAT, HID), f32),
            dma((4,)),
            dma((N_SENDS,)),
            dma((2 * NZ * PARTS,)),
            dma((NZ - 1,)),
            dma((8 * (NZ - 1),)),
            dma((NZ,)),
            dma((NZ,)),
            dma((4 * NZ,)),
            dma((4 * NZ,)),
            dma((NZ,)),
        ],
        compiler_params=pltpu.CompilerParams(
            collective_id=0, has_side_effects=True, vmem_limit_bytes=60 * 2**20
        ),
    )(grad_act, pre_act, inputs, weight)
    return git.T, gw


def solution(mesh):
    return jax.shard_map(
        shards,
        mesh=mesh,
        in_specs=(
            P("gz", ("gy", "gx")),
            P("gz", ("gy", "gx")),
            P("gz", "gx"),
            P("gx", ("gy", "gz")),
        ),
        out_specs=(P("gz", ("gx", "gy")), P("gx", ("gy", "gz"))),
        check_vma=False,
    )
```

```python
import functools

import jax
import jax.numpy as jnp
from jax import lax
from jax.experimental import pallas as pl
from jax.experimental.pallas import tpu as pltpu
from jax.sharding import PartitionSpec as P

MESH = pl.DeviceIdType.MESH
root_half = 0.7071067811865476
inv_root_tau = 0.3989422804014327

TOK, FEAT, HID = 384, 768, 384
NY, NZ, NX = 8, 4, 4
SLICE = FEAT // NY
HALF = SLICE // 2
PARTS = 3
ROWS = TOK // PARTS
ONE_ROW = (1,)


def gelu_grad(grad_act, pre_act):
    value = pre_act.astype(jnp.float32)
    cdf = 0.5 * (1.0 + lax.erf(value * root_half))
    pdf = jnp.exp(-0.5 * value * value) * inv_root_tau
    return (grad_act.astype(jnp.float32) * (cdf + value * pdf)).astype(jnp.bfloat16)


def mod(value, size):
    return lax.rem(value + size, size)


def kernel(
    ga_any, pa_any, inp_any, w_any, git, gw,
    ga, pa, inp, w, gh, ghs, inputs_t, total, pair_out, pair_in, up_out, down_out, up_in, down_in, z_out, z_in, acc,
    load_sem, send_sem, gh_sem, col_sem, ring_sem, core_sem, pair_sem, up_sem, down_sem, z_sem,
):
    loads = [
        pltpu.make_async_copy(src, dst, load_sem.at[i])
        for i, (src, dst) in enumerate(((pa_any, pa), (ga_any, ga), (inp_any, inp), (w_any, w)))
    ]
    for copy in loads:
        copy.start()

    gx, y, gz = (lax.axis_index(name) for name in ("gx", "gy", "gz"))
    zl, x = lax.div(gx, NX), lax.rem(gx, NX)
    zh, c = lax.div(gz, 2), lax.rem(gz, 2)

    def device(x=x, zl=zl, y=y, zh=zh, c=c):
        return (zl * NX + x, y, zh * 2 + c)

    other_core = device(c=1 - c)
    above, below = device(y=mod(y + 1, NY)), device(y=mod(y - 1, NY))
    at_z = [device(zh=mod(zh + k, NZ)) for k in range(NZ)]

    home_zh, home_c = lax.div(x, 2) + 2 * zl, lax.rem(x, 2)
    at_home = jnp.logical_and(home_zh == zh, home_c == c)
    root_x = 2 * lax.rem(zh, 2) + c
    step_x = 2 * c - 1
    role = lax.rem((x - root_x) * step_x + 2 * NX, NX)
    is_root, is_relay = role == 0, role == 1
    onward, backward = device(x=mod(x + step_x, NX)), device(x=mod(x - step_x, NX))

    barrier = pltpu.get_barrier_semaphore()

    def hello(dev):
        pl.semaphore_signal(barrier, inc=1, device_id=dev, device_id_type=MESH)

    other_zl = device(zl=1 - zl)
    for dev in (other_core, above, below, onward, backward, other_zl, at_z[1], at_z[2], at_z[3]):
        hello(dev)

    def first_zl(k, owner_zl):
        return (owner_zl, 1, 1 - owner_zl, 0)[k]

    src_zl = lax.div(zh, 2)
    for k in range(NZ):
        for core in range(2):
            expected = jnp.logical_and(is_root, first_zl(k, src_zl) == zl)
            if k == 0:
                expected = jnp.logical_and(expected, c != core)

            @pl.when(expected)
            def _():
                hello(device(zl=src_zl, zh=mod(zh + k, NZ), c=core))

    @pl.when(jnp.logical_and(is_root, jnp.logical_and(zl != src_zl, c == 1)))
    def _():
        hello(device(zl=src_zl, c=0))

    sends = []

    def remote(src, dst, recv, dev, cond=None):
        copy = pltpu.make_async_remote_copy(
            src_ref=src, dst_ref=dst, send_sem=send_sem.at[len(sends)], recv_sem=recv,
            device_id=dev, device_id_type=MESH,
        )
        sends.append((copy, cond))
        if cond is None:
            copy.start()
        else:
            pl.when(cond)(copy.start)

    def arrived(dst, recv):
        pltpu.make_async_remote_copy(
            src_ref=dst, dst_ref=dst, send_sem=send_sem.at[0], recv_sem=recv,
            device_id=other_core, device_id_type=MESH,
        ).wait_recv()

    loads[0].wait()
    loads[1].wait()
    for r in range(0, TOK, 64):
        gh[r : r + 64, :] = gelu_grad(ga[r : r + 64, :], pa[r : r + 64, :])
    loads[2].wait()
    inputs_t[c, 0] = inp[...].astype(jnp.float32).T.astype(jnp.bfloat16).reshape(NY, SLICE, TOK)
    across = jnp.where(jnp.logical_and(home_zh == zh, c == 0), home_c, 0)
    pl.semaphore_wait(barrier, 10 - at_home.astype(jnp.int32) + across)

    def send_inputs():
        for k in range(1, NZ):
            remote(inputs_t.at[c, 0, y], inputs_t.at[c, k, y], col_sem.at[k - 1], at_z[NZ - k])

    def both(*conds):
        return functools.reduce(jnp.logical_and, conds)

    far = mod(zh - home_zh, NZ)

    def hidden_part(k, core, part):
        return ghs.at[k, core, pl.ds(part * ROWS, ROWS)], gh_sem.at[(2 * k + core) * PARTS + part]

    def send_hidden(turn, direct=False):
        first = jnp.where(far == 0, zl, jnp.where(far == 1, 1, jnp.where(far == 2, 1 - zl, 0)))
        for part in range(PARTS):
            block, sem = hidden_part(far, c, part)
            remote(
                gh.at[pl.ds(part * ROWS, ROWS)], block, sem,
                device(zl=first, zh=home_zh, c=home_c), jnp.logical_and(turn, jnp.logical_not(at_home)),
            )
            if direct:
                remote(
                    gh.at[pl.ds(part * ROWS, ROWS)], block, sem,
                    device(zl=1 - zl, zh=home_zh, c=home_c), both(far == 0, c == 0),
                )

    def keep_hidden():
        @pl.when(at_home)
        def _():
            for part in range(PARTS):
                block, sem = hidden_part(0, c, part)
                pltpu.make_async_copy(gh.at[pl.ds(part * ROWS, ROWS)], block, sem).start()

    def share_inputs():
        remote(inputs_t.at[c, 0], inputs_t.at[c, 0], core_sem.at[0], other_core)

    def piece(k, who, rows=None):
        block = inputs_t.at[c, k, mod(who, NY)]
        return block if rows is None else block.at[pl.ds(rows, HALF)]

    def inputs_ring(step, k):
        up, down = 8 * (k - 1), 8 * (k - 1) + 4
        if step == 0:
            arrived(piece(k, y), col_sem.at[k - 1])
        elif step < 4:
            arrived(piece(k, y - step), ring_sem.at[up + step - 1])
            arrived(piece(k, y + step), ring_sem.at[down + step - 1])
        else:
            arrived(piece(k, y - 4, 0), ring_sem.at[up + 3])
            arrived(piece(k, y + 4, HALF), ring_sem.at[down + 3])
            remote(inputs_t.at[c, k], inputs_t.at[c, k], core_sem.at[k], other_core)
            return
        lo, hi = (0, HALF) if step == 3 else (None, None)
        remote(piece(k, y - step, lo), piece(k, y - step, lo), ring_sem.at[up + step], above)
        remote(piece(k, y + step, hi), piece(k, y + step, hi), ring_sem.at[down + step], below)

    home_row = zl == src_zl
    near = 3 - 2 * zl
    groups = [jnp.where(home_row, *pair) for pair in ((0, near), (near, 0), (4 - near, 2), (2, 4 - near))]
    first_here = (True, home_row, jnp.logical_not(home_row), False)

    def gather(n, who):
        k, first = groups[n], first_here[n]
        for part in range(PARTS):
            for core in range(2):
                block, sem = hidden_part(k, core, part)
                one_row = core in ONE_ROW

                @pl.when(who)
                def _():
                    arrived(block, sem)

                go = who
                if one_row:
                    go = None if first is False else both(who, first)
                if go is not None and (who is is_root or who is is_relay):
                    remote(block, block, sem, onward, go)
                if go is not None and who is is_root:
                    remote(block, block, sem, backward, go)
                if first is not False and (who is is_root or one_row):
                    turn = both(who, first) if one_row else both(who, first, k != 0)
                    remote(block, block, sem, other_zl, turn)

    def product(k, core):
        return lax.dot_general(
            w[...], ghs[k, core], (((1,), (1,)), ((), ())), preferred_element_type=jnp.float32
        ).reshape(NY, SLICE, TOK)

    def compute(n):
        k = groups[n]
        pair_out[k] = product(k, 1 - c).astype(jnp.bfloat16)
        remote(pair_out.at[k], pair_in.at[k], pair_sem.at[k], other_core)
        total[k] = product(k, c)

    def add_pair(n):
        k = groups[n]
        arrived(pair_in.at[k], pair_sem.at[k])
        total[k] = total[k] + pair_in[k].astype(jnp.float32)

    def reduce(n, step):
        k = groups[n]
        for turn in range(2):
            for up in (True, False):
                half = turn if up else 1 - turn
                if step == 1 and turn == 1:
                    continue
                to = mod(y + 5 - step, NY) if up else mod(y - 5 + step, NY)
                out, came, sem = (up_out, up_in, up_sem) if up else (down_out, down_in, down_sem)
                rows = pl.ds(half * HALF, HALF)
                term = total[k, to, rows]
                if step > 2 or (step == 2 and turn == 0):
                    arrived(came.at[k, step - 2, rows], sem.at[8 * k + 2 * (step - 2) + half])
                    term = term + came[k, step - 2, rows].astype(jnp.float32)
                out[k, step - 1, rows] = term.astype(jnp.bfloat16)
                remote(
                    out.at[k, step - 1, rows], came.at[k, step - 1, rows], sem.at[8 * k + 2 * (step - 1) + half],
                    above if up else below,
                )

    def finish(n):
        k = groups[n]
        for half in range(2):
            rows = pl.ds(half * HALF, HALF)
            arrived(up_in.at[k, 3, rows], up_sem.at[8 * k + 6 + half])
            arrived(down_in.at[k, 3, rows], down_sem.at[8 * k + 6 + half])
        whole = total[k, y] + up_in[k, 3].astype(jnp.float32) + down_in[k, 3].astype(jnp.float32)
        total[k, y] = whole
        z_out[k] = whole.astype(jnp.bfloat16)
        remote(z_out.at[k], z_in.at[k], z_sem.at[k], device(zh=mod(zh + k, NZ)), k != 0)

    def weight_grad(n):
        k = groups[n]
        arrived(inputs_t.at[1 - c, k], core_sem.at[k])
        for core in range(2):
            term = lax.dot_general(
                inputs_t[core, k].reshape(FEAT, TOK), ghs[k, core], (((1,), (0,)), ((), ())),
                preferred_element_type=jnp.float32,
            )
            if n == 0 and core == 0:
                acc[...] = term
            else:
                acc[...] += term

    def write_weight_grad():
        gw[...] = acc[...].astype(jnp.bfloat16)

    def write_inputs_grad():
        out = total[0, y]
        for k in range(1, NZ):
            arrived(z_in.at[k], z_sem.at[k])
            out = out + z_in[k].astype(jnp.float32)
        git[...] = out.astype(jnp.bfloat16)

    loads[3].wait()
    root, relay, role2, role3 = is_root, is_relay, role == 2, role == 3
    schedule = (
        (send_inputs,), (keep_hidden,), (send_hidden, far != 2, True), (share_inputs,), (gather, 0, root),
        (inputs_ring, 0, 1), (inputs_ring, 0, 3), (inputs_ring, 0, 2), (gather, 1, root), (send_hidden, both(far == 2, root)), (gather, 0, role3), (send_hidden, both(far == 2, role3)),
        (gather, 0, relay), (inputs_ring, 1, 1), (inputs_ring, 1, 3), (inputs_ring, 1, 2), (gather, 0, role2),
        (compute, 0), (gather, 2, root), (gather, 1, relay), (add_pair, 0), (reduce, 0, 1), (inputs_ring, 2, 1), (inputs_ring, 2, 3), (inputs_ring, 2, 2),
        (gather, 3, root), (gather, 1, role2), (gather, 1, role3), (compute, 1), (gather, 2, relay), (reduce, 0, 2), (inputs_ring, 3, 1), (inputs_ring, 3, 3), (inputs_ring, 3, 2),
        (add_pair, 1), (reduce, 1, 1), (reduce, 0, 3), (gather, 2, role2), (gather, 2, role3), (compute, 2), (inputs_ring, 4, 1), (inputs_ring, 4, 3), (inputs_ring, 4, 2),
        (gather, 3, relay), (reduce, 1, 2), (reduce, 0, 4), (add_pair, 2), (reduce, 2, 1), (reduce, 1, 3),
        (finish, 0), (gather, 3, role2), (gather, 3, role3), (compute, 3), (reduce, 2, 2), (reduce, 1, 4), (add_pair, 3), (reduce, 3, 1),
        (reduce, 2, 3), (finish, 1), (weight_grad, 0), (reduce, 3, 2), (reduce, 2, 4), (weight_grad, 1),
        (reduce, 3, 3), (finish, 2), (weight_grad, 2), (reduce, 3, 4), (weight_grad, 3), (write_weight_grad,),
        (finish, 3), (write_inputs_grad,),
    )
    for step, *args in schedule:
        step(*args)

    for copy, cond in sends:
        if cond is None:
            copy.wait_send()
        else:
            pl.when(cond)(copy.wait_send)


N_SENDS = 320


def shards(grad_act, pre_act, inputs, weight):
    vmem = pl.BlockSpec(memory_space=pltpu.VMEM)
    bf16, f32 = jnp.bfloat16, jnp.float32
    dma = pltpu.SemaphoreType.DMA
    git, gw = pl.pallas_call(
        kernel,
        out_shape=(
            jax.ShapeDtypeStruct((SLICE, TOK), bf16),
            jax.ShapeDtypeStruct((FEAT, HID), bf16),
        ),
        in_specs=[pl.BlockSpec(memory_space=pl.ANY)] * 4,
        out_specs=(vmem, vmem),
        scratch_shapes=[
            pltpu.VMEM((TOK, HID), bf16),
            pltpu.VMEM((TOK, HID), bf16),
            pltpu.VMEM((TOK, FEAT), bf16),
            pltpu.VMEM((FEAT, HID), bf16),
            pltpu.VMEM((TOK, HID), bf16),
            pltpu.VMEM((NZ, 2, TOK, HID), bf16),
            pltpu.VMEM((2, NZ, NY, SLICE, TOK), bf16),
            pltpu.VMEM((NZ, NY, SLICE, TOK), f32),
            pltpu.VMEM((NZ, NY, SLICE, TOK), bf16),
            pltpu.VMEM((NZ, NY, SLICE, TOK), bf16),
            pltpu.VMEM((NZ, 4, SLICE, TOK), bf16),
            pltpu.VMEM((NZ, 4, SLICE, TOK), bf16),
            pltpu.VMEM((NZ, 4, SLICE, TOK), bf16),
            pltpu.VMEM((NZ, 4, SLICE, TOK), bf16),
            pltpu.VMEM((NZ, SLICE, TOK), bf16),
            pltpu.VMEM((NZ, SLICE, TOK), bf16),
            pltpu.VMEM((FEAT, HID), f32),
            dma((4,)),
            dma((N_SENDS,)),
            dma((2 * NZ * PARTS,)),
            dma((NZ - 1,)),
            dma((8 * (NZ - 1),)),
            dma((NZ,)),
            dma((NZ,)),
            dma((8 * NZ,)),
            dma((8 * NZ,)),
            dma((NZ,)),
        ],
        compiler_params=pltpu.CompilerParams(
            collective_id=0, has_side_effects=True, vmem_limit_bytes=60 * 2**20
        ),
    )(grad_act, pre_act, inputs, weight)
    return git.T, gw


def solution(mesh):
    return jax.shard_map(
        shards,
        mesh=mesh,
        in_specs=(
            P("gz", ("gy", "gx")),
            P("gz", ("gy", "gx")),
            P("gz", "gx"),
            P("gx", ("gy", "gz")),
        ),
        out_specs=(P("gz", ("gx", "gy")), P("gx", ("gy", "gz"))),
        check_vma=False,
    )
```

```python
import functools

import jax
import jax.numpy as jnp
from jax import lax
from jax.experimental import pallas as pl
from jax.experimental.pallas import tpu as pltpu
from jax.sharding import PartitionSpec as P

MESH = pl.DeviceIdType.MESH
root_half = 0.7071067811865476
inv_root_tau = 0.3989422804014327

TOK, FEAT, HID = 384, 768, 384
NY, NZ, NX = 8, 4, 4
SLICE = FEAT // NY
HALF = SLICE // 2
PARTS = 3
ROWS = TOK // PARTS
ONE_ROW = (1,)


def gelu_grad(grad_act, pre_act):
    value = pre_act.astype(jnp.float32)
    cdf = 0.5 * (1.0 + lax.erf(value * root_half))
    pdf = jnp.exp(-0.5 * value * value) * inv_root_tau
    return (grad_act.astype(jnp.float32) * (cdf + value * pdf)).astype(jnp.bfloat16)


def mod(value, size):
    return lax.rem(value + size, size)


def kernel(
    ga_any, pa_any, inp_any, w_any, git, gw,
    ga, pa, inp, w, gh, ghs, inputs_t, total, pair_out, pair_in, up_out, down_out, up_in, down_in, z_out, z_in, acc,
    load_sem, send_sem, gh_sem, col_sem, ring_sem, core_sem, pair_sem, up_sem, down_sem, z_sem,
):
    loads = [
        pltpu.make_async_copy(src, dst, load_sem.at[i])
        for i, (src, dst) in enumerate(((pa_any, pa), (ga_any, ga), (inp_any, inp), (w_any, w)))
    ]
    for copy in loads:
        copy.start()

    gx, y, gz = (lax.axis_index(name) for name in ("gx", "gy", "gz"))
    zl, x = lax.div(gx, NX), lax.rem(gx, NX)
    zh, c = lax.div(gz, 2), lax.rem(gz, 2)

    def device(x=x, zl=zl, y=y, zh=zh, c=c):
        return (zl * NX + x, y, zh * 2 + c)

    other_core = device(c=1 - c)
    above, below = device(y=mod(y + 1, NY)), device(y=mod(y - 1, NY))
    at_z = [device(zh=mod(zh + k, NZ)) for k in range(NZ)]

    home_zh, home_c = lax.div(x, 2) + 2 * zl, lax.rem(x, 2)
    at_home = jnp.logical_and(home_zh == zh, home_c == c)
    root_x = 2 * lax.rem(zh, 2) + c
    step_x = 2 * c - 1
    role = lax.rem((x - root_x) * step_x + 2 * NX, NX)
    is_root, is_relay = role == 0, role == 1
    onward, backward = device(x=mod(x + step_x, NX)), device(x=mod(x - step_x, NX))

    barrier = pltpu.get_barrier_semaphore()

    def hello(dev):
        pl.semaphore_signal(barrier, inc=1, device_id=dev, device_id_type=MESH)

    other_zl = device(zl=1 - zl)
    for dev in (other_core, above, below, onward, backward, other_zl, at_z[1], at_z[2], at_z[3]):
        hello(dev)

    def first_zl(k, owner_zl):
        return (owner_zl, 1, 1 - owner_zl, 0)[k]

    src_zl = lax.div(zh, 2)
    for k in range(NZ):
        for core in range(2):
            expected = jnp.logical_and(is_root, first_zl(k, src_zl) == zl)
            if k == 0:
                expected = jnp.logical_and(expected, c != core)

            @pl.when(expected)
            def _():
                hello(device(zl=src_zl, zh=mod(zh + k, NZ), c=core))

    @pl.when(jnp.logical_and(is_root, jnp.logical_and(zl != src_zl, c == 1)))
    def _():
        hello(device(zl=src_zl, c=0))

    sends = []

    def remote(src, dst, recv, dev, cond=None):
        copy = pltpu.make_async_remote_copy(
            src_ref=src, dst_ref=dst, send_sem=send_sem.at[len(sends)], recv_sem=recv,
            device_id=dev, device_id_type=MESH,
        )
        sends.append((copy, cond))
        if cond is None:
            copy.start()
        else:
            pl.when(cond)(copy.start)

    def arrived(dst, recv):
        pltpu.make_async_remote_copy(
            src_ref=dst, dst_ref=dst, send_sem=send_sem.at[0], recv_sem=recv,
            device_id=other_core, device_id_type=MESH,
        ).wait_recv()

    loads[0].wait()
    loads[1].wait()
    for r in range(0, TOK, 64):
        gh[r : r + 64, :] = gelu_grad(ga[r : r + 64, :], pa[r : r + 64, :])
    loads[2].wait()
    inputs_t[c, 0] = inp[...].astype(jnp.float32).T.astype(jnp.bfloat16).reshape(NY, SLICE, TOK)
    across = jnp.where(jnp.logical_and(home_zh == zh, c == 0), home_c, 0)
    pl.semaphore_wait(barrier, 10 - at_home.astype(jnp.int32) + across)

    def send_inputs():
        for k in range(1, NZ):
            remote(inputs_t.at[c, 0, y], inputs_t.at[c, k, y], col_sem.at[k - 1], at_z[NZ - k])

    def both(*conds):
        return functools.reduce(jnp.logical_and, conds)

    far = mod(zh - home_zh, NZ)

    def hidden_part(k, core, part):
        return ghs.at[k, core, pl.ds(part * ROWS, ROWS)], gh_sem.at[(2 * k + core) * PARTS + part]

    def send_hidden(turn, direct=False):
        first = jnp.where(far == 0, zl, jnp.where(far == 1, 1, jnp.where(far == 2, 1 - zl, 0)))
        for part in range(PARTS):
            block, sem = hidden_part(far, c, part)
            remote(
                gh.at[pl.ds(part * ROWS, ROWS)], block, sem,
                device(zl=first, zh=home_zh, c=home_c), jnp.logical_and(turn, jnp.logical_not(at_home)),
            )
            if direct:
                remote(
                    gh.at[pl.ds(part * ROWS, ROWS)], block, sem,
                    device(zl=1 - zl, zh=home_zh, c=home_c), both(far == 0, c == 0),
                )

    def keep_hidden():
        @pl.when(at_home)
        def _():
            for part in range(PARTS):
                block, sem = hidden_part(0, c, part)
                pltpu.make_async_copy(gh.at[pl.ds(part * ROWS, ROWS)], block, sem).start()

    def share_inputs():
        remote(inputs_t.at[c, 0], inputs_t.at[c, 0], core_sem.at[0], other_core)

    def piece(k, who, rows=None):
        block = inputs_t.at[c, k, mod(who, NY)]
        return block if rows is None else block.at[pl.ds(rows, HALF)]

    def inputs_ring(step, k):
        up, down = 8 * (k - 1), 8 * (k - 1) + 4
        if step == 0:
            arrived(piece(k, y), col_sem.at[k - 1])
        elif step < 4:
            arrived(piece(k, y - step), ring_sem.at[up + step - 1])
            arrived(piece(k, y + step), ring_sem.at[down + step - 1])
        else:
            arrived(piece(k, y - 4, 0), ring_sem.at[up + 3])
            arrived(piece(k, y + 4, HALF), ring_sem.at[down + 3])
            remote(inputs_t.at[c, k], inputs_t.at[c, k], core_sem.at[k], other_core)
            return
        lo, hi = (0, HALF) if step == 3 else (None, None)
        remote(piece(k, y - step, lo), piece(k, y - step, lo), ring_sem.at[up + step], above)
        remote(piece(k, y + step, hi), piece(k, y + step, hi), ring_sem.at[down + step], below)

    home_row = zl == src_zl
    near = 3 - 2 * zl
    groups = [jnp.where(home_row, *pair) for pair in ((0, near), (near, 0), (4 - near, 2), (2, 4 - near))]
    first_here = (True, home_row, jnp.logical_not(home_row), False)

    def gather(n, who):
        k, first = groups[n], first_here[n]
        for part in range(PARTS):
            for core in range(2):
                block, sem = hidden_part(k, core, part)
                one_row = core in ONE_ROW

                @pl.when(who)
                def _():
                    arrived(block, sem)

                go = who
                if one_row:
                    go = None if first is False else both(who, first)
                if go is not None and (who is is_root or who is is_relay):
                    remote(block, block, sem, onward, go)
                if go is not None and who is is_root:
                    remote(block, block, sem, backward, go)
                if first is not False and (who is is_root or one_row):
                    turn = both(who, first) if one_row else both(who, first, k != 0)
                    remote(block, block, sem, other_zl, turn)

    def product(k, core, half):
        rows = FEAT // 2
        return lax.dot_general(
            w[half * rows : (half + 1) * rows, :], ghs[k, core], (((1,), (1,)), ((), ())),
            preferred_element_type=jnp.float32,
        ).reshape(NY // 2, SLICE, TOK)

    def compute(n):
        k = groups[n]
        for half in range(2):
            some = pl.ds(half * (NY // 2), NY // 2)
            pair_out[k, some] = product(k, 1 - c, half).astype(jnp.bfloat16)
            remote(pair_out.at[k, some], pair_in.at[k, some], pair_sem.at[2 * k + half], other_core)
        for half in range(2):
            total[k, pl.ds(half * (NY // 2), NY // 2)] = product(k, c, half)

    def add_pair(n):
        k = groups[n]
        for half in range(2):
            some = pl.ds(half * (NY // 2), NY // 2)
            arrived(pair_in.at[k, some], pair_sem.at[2 * k + half])
            total[k, some] = total[k, some] + pair_in[k, some].astype(jnp.float32)

    def reduce(n, step):
        k = groups[n]
        for turn in range(2):
            for up in (True, False):
                half = turn if up else 1 - turn
                if step == 1 and turn == 1:
                    continue
                to = mod(y + 5 - step, NY) if up else mod(y - 5 + step, NY)
                out, came, sem = (up_out, up_in, up_sem) if up else (down_out, down_in, down_sem)
                rows = pl.ds(half * HALF, HALF)
                term = total[k, to, rows]
                if step > 2 or (step == 2 and turn == 0):
                    arrived(came.at[k, step - 2, rows], sem.at[8 * k + 2 * (step - 2) + half])
                    term = term + came[k, step - 2, rows].astype(jnp.float32)
                out[k, step - 1, rows] = term.astype(jnp.bfloat16)
                remote(
                    out.at[k, step - 1, rows], came.at[k, step - 1, rows], sem.at[8 * k + 2 * (step - 1) + half],
                    above if up else below,
                )

    def finish(n):
        k = groups[n]
        for half in range(2):
            rows = pl.ds(half * HALF, HALF)
            arrived(up_in.at[k, 3, rows], up_sem.at[8 * k + 6 + half])
            arrived(down_in.at[k, 3, rows], down_sem.at[8 * k + 6 + half])
        whole = total[k, y] + up_in[k, 3].astype(jnp.float32) + down_in[k, 3].astype(jnp.float32)
        total[k, y] = whole
        z_out[k] = whole.astype(jnp.bfloat16)
        remote(z_out.at[k], z_in.at[k], z_sem.at[k], device(zh=mod(zh + k, NZ)), k != 0)

    def weight_grad(n):
        k = groups[n]
        arrived(inputs_t.at[1 - c, k], core_sem.at[k])
        for core in range(2):
            term = lax.dot_general(
                inputs_t[core, k].reshape(FEAT, TOK), ghs[k, core], (((1,), (0,)), ((), ())),
                preferred_element_type=jnp.float32,
            )
            if n == 0 and core == 0:
                acc[...] = term
            else:
                acc[...] += term

    def write_weight_grad():
        gw[...] = acc[...].astype(jnp.bfloat16)

    def write_inputs_grad():
        out = total[0, y]
        for k in range(1, NZ):
            arrived(z_in.at[k], z_sem.at[k])
            out = out + z_in[k].astype(jnp.float32)
        git[...] = out.astype(jnp.bfloat16)

    loads[3].wait()
    root, relay, role2, role3 = is_root, is_relay, role == 2, role == 3
    schedule = (
        (send_inputs,), (keep_hidden,), (send_hidden, far != 2, True), (share_inputs,), (gather, 0, root),
        (inputs_ring, 0, 1), (inputs_ring, 0, 3), (inputs_ring, 0, 2), (gather, 1, root), (send_hidden, both(far == 2, root)), (gather, 0, role3), (send_hidden, both(far == 2, role3)),
        (gather, 0, relay), (inputs_ring, 1, 1), (inputs_ring, 1, 3), (inputs_ring, 1, 2), (gather, 0, role2),
        (compute, 0), (gather, 2, root), (gather, 1, relay), (add_pair, 0), (reduce, 0, 1), (inputs_ring, 2, 1), (inputs_ring, 2, 3), (inputs_ring, 2, 2),
        (gather, 3, root), (gather, 1, role2), (gather, 1, role3), (compute, 1), (gather, 2, relay), (reduce, 0, 2), (inputs_ring, 3, 1), (inputs_ring, 3, 3), (inputs_ring, 3, 2),
        (add_pair, 1), (reduce, 1, 1), (reduce, 0, 3), (gather, 2, role2), (gather, 2, role3), (compute, 2), (inputs_ring, 4, 1), (inputs_ring, 4, 3), (inputs_ring, 4, 2),
        (gather, 3, relay), (reduce, 1, 2), (reduce, 0, 4), (add_pair, 2), (reduce, 2, 1), (reduce, 1, 3),
        (finish, 0), (gather, 3, role2), (gather, 3, role3), (compute, 3), (reduce, 2, 2), (reduce, 1, 4), (add_pair, 3), (reduce, 3, 1),
        (reduce, 2, 3), (finish, 1), (weight_grad, 0), (reduce, 3, 2), (reduce, 2, 4), (weight_grad, 1),
        (reduce, 3, 3), (finish, 2), (weight_grad, 2), (reduce, 3, 4), (weight_grad, 3), (write_weight_grad,),
        (finish, 3), (write_inputs_grad,),
    )
    for step, *args in schedule:
        step(*args)

    for copy, cond in sends:
        if cond is None:
            copy.wait_send()
        else:
            pl.when(cond)(copy.wait_send)


N_SENDS = 320


def shards(grad_act, pre_act, inputs, weight):
    vmem = pl.BlockSpec(memory_space=pltpu.VMEM)
    bf16, f32 = jnp.bfloat16, jnp.float32
    dma = pltpu.SemaphoreType.DMA
    git, gw = pl.pallas_call(
        kernel,
        out_shape=(
            jax.ShapeDtypeStruct((SLICE, TOK), bf16),
            jax.ShapeDtypeStruct((FEAT, HID), bf16),
        ),
        in_specs=[pl.BlockSpec(memory_space=pl.ANY)] * 4,
        out_specs=(vmem, vmem),
        scratch_shapes=[
            pltpu.VMEM((TOK, HID), bf16),
            pltpu.VMEM((TOK, HID), bf16),
            pltpu.VMEM((TOK, FEAT), bf16),
            pltpu.VMEM((FEAT, HID), bf16),
            pltpu.VMEM((TOK, HID), bf16),
            pltpu.VMEM((NZ, 2, TOK, HID), bf16),
            pltpu.VMEM((2, NZ, NY, SLICE, TOK), bf16),
            pltpu.VMEM((NZ, NY, SLICE, TOK), f32),
            pltpu.VMEM((NZ, NY, SLICE, TOK), bf16),
            pltpu.VMEM((NZ, NY, SLICE, TOK), bf16),
            pltpu.VMEM((NZ, 4, SLICE, TOK), bf16),
            pltpu.VMEM((NZ, 4, SLICE, TOK), bf16),
            pltpu.VMEM((NZ, 4, SLICE, TOK), bf16),
            pltpu.VMEM((NZ, 4, SLICE, TOK), bf16),
            pltpu.VMEM((NZ, SLICE, TOK), bf16),
            pltpu.VMEM((NZ, SLICE, TOK), bf16),
            pltpu.VMEM((FEAT, HID), f32),
            dma((4,)),
            dma((N_SENDS,)),
            dma((2 * NZ * PARTS,)),
            dma((NZ - 1,)),
            dma((8 * (NZ - 1),)),
            dma((NZ,)),
            dma((2 * NZ,)),
            dma((8 * NZ,)),
            dma((8 * NZ,)),
            dma((NZ,)),
        ],
        compiler_params=pltpu.CompilerParams(
            collective_id=0, has_side_effects=True, vmem_limit_bytes=60 * 2**20
        ),
    )(grad_act, pre_act, inputs, weight)
    return git.T, gw


def solution(mesh):
    return jax.shard_map(
        shards,
        mesh=mesh,
        in_specs=(
            P("gz", ("gy", "gx")),
            P("gz", ("gy", "gx")),
            P("gz", "gx"),
            P("gx", ("gy", "gz")),
        ),
        out_specs=(P("gz", ("gx", "gy")), P("gx", ("gy", "gz"))),
        check_vma=False,
    )
```

```python
import functools

import jax
import jax.numpy as jnp
from jax import lax
from jax.experimental import pallas as pl
from jax.experimental.pallas import tpu as pltpu
from jax.sharding import PartitionSpec as P

MESH = pl.DeviceIdType.MESH
root_half = 0.7071067811865476
inv_root_tau = 0.3989422804014327

TOK, FEAT, HID = 384, 768, 384
NY, NZ, NX = 8, 4, 4
SLICE = FEAT // NY
HALF = SLICE // 2
PARTS = 3
ROWS = TOK // PARTS
ONE_ROW = (1,)


def gelu_grad(grad_act, pre_act):
    value = pre_act.astype(jnp.float32)
    cdf = 0.5 * (1.0 + lax.erf(value * root_half))
    pdf = jnp.exp(-0.5 * value * value) * inv_root_tau
    return (grad_act.astype(jnp.float32) * (cdf + value * pdf)).astype(jnp.bfloat16)


def mod(value, size):
    return lax.rem(value + size, size)


def kernel(
    ga_any, pa_any, inp_any, w_any, git, gw,
    ga, pa, inp, w, gh, ghs, inputs_t, total, pair_out, pair_in, up_out, down_out, up_in, down_in, z_out, z_in, acc,
    load_sem, send_sem, gh_sem, col_sem, ring_sem, core_sem, pair_sem, up_sem, down_sem, z_sem,
):
    loads = [
        pltpu.make_async_copy(src, dst, load_sem.at[i])
        for i, (src, dst) in enumerate(((pa_any, pa), (ga_any, ga), (inp_any, inp), (w_any, w)))
    ]
    for copy in loads:
        copy.start()

    gx, y, gz = (lax.axis_index(name) for name in ("gx", "gy", "gz"))
    zl, x = lax.div(gx, NX), lax.rem(gx, NX)
    zh, c = lax.div(gz, 2), lax.rem(gz, 2)

    def device(x=x, zl=zl, y=y, zh=zh, c=c):
        return (zl * NX + x, y, zh * 2 + c)

    other_core = device(c=1 - c)
    above, below = device(y=mod(y + 1, NY)), device(y=mod(y - 1, NY))
    at_z = [device(zh=mod(zh + k, NZ)) for k in range(NZ)]

    home_zh, home_c = lax.div(x, 2) + 2 * zl, lax.rem(x, 2)
    at_home = jnp.logical_and(home_zh == zh, home_c == c)
    root_x = 2 * lax.rem(zh, 2) + c
    step_x = 2 * c - 1
    role = lax.rem((x - root_x) * step_x + 2 * NX, NX)
    is_root, is_relay = role == 0, role == 1
    onward, backward = device(x=mod(x + step_x, NX)), device(x=mod(x - step_x, NX))

    barrier = pltpu.get_barrier_semaphore()

    def hello(dev):
        pl.semaphore_signal(barrier, inc=1, device_id=dev, device_id_type=MESH)

    other_zl = device(zl=1 - zl)
    for dev in (other_core, above, below, onward, backward, other_zl, at_z[1], at_z[2], at_z[3]):
        hello(dev)

    def first_zl(k, owner_zl):
        return (owner_zl, 1, 1 - owner_zl, 0)[k]

    src_zl = lax.div(zh, 2)
    for k in range(NZ):
        for core in range(2):
            expected = jnp.logical_and(is_root, first_zl(k, src_zl) == zl)
            if k == 0:
                expected = jnp.logical_and(expected, c != core)

            @pl.when(expected)
            def _():
                hello(device(zl=src_zl, zh=mod(zh + k, NZ), c=core))

    @pl.when(jnp.logical_and(is_root, jnp.logical_and(zl != src_zl, c == 1)))
    def _():
        hello(device(zl=src_zl, c=0))

    sends = []

    def remote(src, dst, recv, dev, cond=None):
        copy = pltpu.make_async_remote_copy(
            src_ref=src, dst_ref=dst, send_sem=send_sem.at[len(sends)], recv_sem=recv,
            device_id=dev, device_id_type=MESH,
        )
        sends.append((copy, cond))
        if cond is None:
            copy.start()
        else:
            pl.when(cond)(copy.start)

    def arrived(dst, recv):
        pltpu.make_async_remote_copy(
            src_ref=dst, dst_ref=dst, send_sem=send_sem.at[0], recv_sem=recv,
            device_id=other_core, device_id_type=MESH,
        ).wait_recv()

    loads[0].wait()
    loads[1].wait()
    for r in range(0, TOK, 64):
        gh[r : r + 64, :] = gelu_grad(ga[r : r + 64, :], pa[r : r + 64, :])
    loads[2].wait()
    inputs_t[c, 0] = inp[...].astype(jnp.float32).T.astype(jnp.bfloat16).reshape(NY, SLICE, TOK)
    across = jnp.where(jnp.logical_and(home_zh == zh, c == 0), home_c, 0)
    pl.semaphore_wait(barrier, 10 - at_home.astype(jnp.int32) + across)

    def send_inputs():
        for k in range(1, NZ):
            remote(inputs_t.at[c, 0, y], inputs_t.at[c, k, y], col_sem.at[k - 1], at_z[NZ - k])

    def both(*conds):
        return functools.reduce(jnp.logical_and, conds)

    far = mod(zh - home_zh, NZ)

    def hidden_part(k, core, part):
        return ghs.at[k, core, pl.ds(part * ROWS, ROWS)], gh_sem.at[(2 * k + core) * PARTS + part]

    def send_hidden(turn, direct=False):
        first = jnp.where(far == 0, zl, jnp.where(far == 1, 1, jnp.where(far == 2, 1 - zl, 0)))
        for part in range(PARTS):
            block, sem = hidden_part(far, c, part)
            remote(
                gh.at[pl.ds(part * ROWS, ROWS)], block, sem,
                device(zl=first, zh=home_zh, c=home_c), jnp.logical_and(turn, jnp.logical_not(at_home)),
            )
            if direct:
                remote(
                    gh.at[pl.ds(part * ROWS, ROWS)], block, sem,
                    device(zl=1 - zl, zh=home_zh, c=home_c), both(far == 0, c == 0),
                )

    def keep_hidden():
        @pl.when(at_home)
        def _():
            for part in range(PARTS):
                block, sem = hidden_part(0, c, part)
                pltpu.make_async_copy(gh.at[pl.ds(part * ROWS, ROWS)], block, sem).start()

    def share_inputs():
        remote(inputs_t.at[c, 0], inputs_t.at[c, 0], core_sem.at[0], other_core)

    def piece(k, who, rows=None):
        block = inputs_t.at[c, k, mod(who, NY)]
        return block if rows is None else block.at[pl.ds(rows, HALF)]

    def inputs_ring(step, k):
        up, down = 8 * (k - 1), 8 * (k - 1) + 4
        if step == 0:
            arrived(piece(k, y), col_sem.at[k - 1])
        elif step < 4:
            arrived(piece(k, y - step), ring_sem.at[up + step - 1])
            arrived(piece(k, y + step), ring_sem.at[down + step - 1])
        else:
            arrived(piece(k, y - 4, 0), ring_sem.at[up + 3])
            arrived(piece(k, y + 4, HALF), ring_sem.at[down + 3])
            remote(inputs_t.at[c, k], inputs_t.at[c, k], core_sem.at[k], other_core)
            return
        lo, hi = (0, HALF) if step == 3 else (None, None)
        remote(piece(k, y - step, lo), piece(k, y - step, lo), ring_sem.at[up + step], above)
        remote(piece(k, y + step, hi), piece(k, y + step, hi), ring_sem.at[down + step], below)

    home_row = zl == src_zl
    near = 3 - 2 * zl
    groups = [jnp.where(home_row, *pair) for pair in ((0, near), (near, 0), (4 - near, 2), (2, 4 - near))]
    first_here = (True, home_row, jnp.logical_not(home_row), False)

    def gather(n, who):
        k, first = groups[n], first_here[n]
        for part in range(PARTS):
            for core in range(2):
                block, sem = hidden_part(k, core, part)
                one_row = core in ONE_ROW

                @pl.when(who)
                def _():
                    arrived(block, sem)

                go = who
                if one_row:
                    go = None if first is False else both(who, first)
                if go is not None and (who is is_root or who is is_relay):
                    remote(block, block, sem, onward, go)
                if go is not None and who is is_root:
                    remote(block, block, sem, backward, go)
                if first is not False and (who is is_root or one_row):
                    turn = both(who, first) if one_row else both(who, first, k != 0)
                    remote(block, block, sem, other_zl, turn)

    def product(k, core):
        return lax.dot_general(
            w[...], ghs[k, core], (((1,), (1,)), ((), ())), preferred_element_type=jnp.float32
        ).reshape(NY, SLICE, TOK)

    def compute(n):
        k = groups[n]
        pair_out[k] = product(k, 1 - c).astype(jnp.bfloat16)
        remote(pair_out.at[k], pair_in.at[k], pair_sem.at[k], other_core)
        total[k] = product(k, c)

    def add_pair(n):
        k = groups[n]
        arrived(pair_in.at[k], pair_sem.at[k])
        total[k] = total[k] + pair_in[k].astype(jnp.float32)

    def reduce(n, step):
        k = groups[n]
        up_to, down_to = mod(y + 5 - step, NY), mod(y - 5 + step, NY)
        up_dst, down_dst = up_in.at[k, step - 1], down_in.at[k, step - 1]
        up_src, down_src = up_out.at[k, step - 1], down_out.at[k, step - 1]
        lo, hi = pl.ds(0, HALF), pl.ds(HALF, HALF)
        if step == 1:
            up_out[k, 0, lo] = total[k, up_to, lo].astype(jnp.bfloat16)
            down_out[k, 0, hi] = total[k, down_to, hi].astype(jnp.bfloat16)
            up_src, up_dst = up_src.at[lo], up_dst.at[lo]
            down_src, down_dst = down_src.at[hi], down_dst.at[hi]
        elif step == 2:
            arrived(up_in.at[k, 0, lo], up_sem.at[4 * k])
            up_out[k, 1, lo] = (total[k, up_to, lo] + up_in[k, 0, lo].astype(jnp.float32)).astype(jnp.bfloat16)
            up_out[k, 1, hi] = total[k, up_to, hi].astype(jnp.bfloat16)
            arrived(down_in.at[k, 0, hi], down_sem.at[4 * k])
            down_out[k, 1, hi] = (total[k, down_to, hi] + down_in[k, 0, hi].astype(jnp.float32)).astype(jnp.bfloat16)
            down_out[k, 1, lo] = total[k, down_to, lo].astype(jnp.bfloat16)
        else:
            arrived(up_in.at[k, step - 2], up_sem.at[4 * k + step - 2])
            up_out[k, step - 1] = (total[k, up_to] + up_in[k, step - 2].astype(jnp.float32)).astype(jnp.bfloat16)
            arrived(down_in.at[k, step - 2], down_sem.at[4 * k + step - 2])
            down_out[k, step - 1] = (total[k, down_to] + down_in[k, step - 2].astype(jnp.float32)).astype(jnp.bfloat16)
        remote(up_src, up_dst, up_sem.at[4 * k + step - 1], above)
        remote(down_src, down_dst, down_sem.at[4 * k + step - 1], below)

    def finish(n):
        k = groups[n]
        arrived(up_in.at[k, 3], up_sem.at[4 * k + 3])
        arrived(down_in.at[k, 3], down_sem.at[4 * k + 3])
        whole = total[k, y] + up_in[k, 3].astype(jnp.float32) + down_in[k, 3].astype(jnp.float32)
        total[k, y] = whole
        z_out[k] = whole.astype(jnp.bfloat16)
        remote(z_out.at[k], z_in.at[k], z_sem.at[k], device(zh=mod(zh + k, NZ)), k != 0)

    def weight_grad(n):
        k = groups[n]
        arrived(inputs_t.at[1 - c, k], core_sem.at[k])
        for core in range(2):
            term = lax.dot_general(
                inputs_t[core, k].reshape(FEAT, TOK), ghs[k, core], (((1,), (0,)), ((), ())),
                preferred_element_type=jnp.float32,
            )
            if n == 0 and core == 0:
                acc[...] = term
            else:
                acc[...] += term

    def write_weight_grad():
        gw[...] = acc[...].astype(jnp.bfloat16)

    def write_inputs_grad():
        out = total[0, y]
        for k in range(1, NZ):
            arrived(z_in.at[k], z_sem.at[k])
            out = out + z_in[k].astype(jnp.float32)
        git[...] = out.astype(jnp.bfloat16)

    loads[3].wait()
    root, relay, role2, role3 = is_root, is_relay, role == 2, role == 3
    schedule = (
        (send_inputs,), (keep_hidden,), (send_hidden, far != 2, True), (share_inputs,), (gather, 0, root),
        (inputs_ring, 0, 1), (inputs_ring, 0, 3), (inputs_ring, 0, 2), (gather, 1, root), (send_hidden, both(far == 2, root)), (gather, 0, role3), (send_hidden, both(far == 2, role3)),
        (gather, 0, relay), (inputs_ring, 1, 1), (inputs_ring, 1, 3), (inputs_ring, 1, 2), (gather, 0, role2),
        (compute, 0), (gather, 2, root), (gather, 1, relay), (add_pair, 0), (reduce, 0, 1), (inputs_ring, 2, 1), (inputs_ring, 2, 3), (inputs_ring, 2, 2),
        (gather, 3, root), (gather, 1, role2), (gather, 1, role3), (compute, 1), (gather, 2, relay), (reduce, 0, 2), (inputs_ring, 3, 1), (inputs_ring, 3, 3), (inputs_ring, 3, 2),
        (add_pair, 1), (reduce, 1, 1), (reduce, 0, 3), (gather, 2, role2), (gather, 2, role3), (compute, 2), (inputs_ring, 4, 1), (inputs_ring, 4, 3), (inputs_ring, 4, 2),
        (gather, 3, relay), (reduce, 1, 2), (reduce, 0, 4), (add_pair, 2), (reduce, 2, 1), (reduce, 1, 3),
        (finish, 0), (gather, 3, role2), (gather, 3, role3), (compute, 3), (reduce, 2, 2), (reduce, 1, 4), (add_pair, 3), (reduce, 3, 1),
        (reduce, 2, 3), (finish, 1), (weight_grad, 0), (reduce, 3, 2), (reduce, 2, 4), (weight_grad, 1),
        (reduce, 3, 3), (finish, 2), (weight_grad, 2), (reduce, 3, 4), (weight_grad, 3), (write_weight_grad,),
        (finish, 3), (write_inputs_grad,),
    )
    for step, *args in schedule:
        step(*args)

    for copy, cond in sends:
        if cond is None:
            copy.wait_send()
        else:
            pl.when(cond)(copy.wait_send)


N_SENDS = 320


def shards(grad_act, pre_act, inputs, weight):
    vmem = pl.BlockSpec(memory_space=pltpu.VMEM)
    bf16, f32 = jnp.bfloat16, jnp.float32
    dma = pltpu.SemaphoreType.DMA
    git, gw = pl.pallas_call(
        kernel,
        out_shape=(
            jax.ShapeDtypeStruct((SLICE, TOK), bf16),
            jax.ShapeDtypeStruct((FEAT, HID), bf16),
        ),
        in_specs=[pl.BlockSpec(memory_space=pl.ANY)] * 4,
        out_specs=(vmem, vmem),
        scratch_shapes=[
            pltpu.VMEM((TOK, HID), bf16),
            pltpu.VMEM((TOK, HID), bf16),
            pltpu.VMEM((TOK, FEAT), bf16),
            pltpu.VMEM((FEAT, HID), bf16),
            pltpu.VMEM((TOK, HID), bf16),
            pltpu.VMEM((NZ, 2, TOK, HID), bf16),
            pltpu.VMEM((2, NZ, NY, SLICE, TOK), bf16),
            pltpu.VMEM((NZ, NY, SLICE, TOK), f32),
            pltpu.VMEM((NZ, NY, SLICE, TOK), bf16),
            pltpu.VMEM((NZ, NY, SLICE, TOK), bf16),
            pltpu.VMEM((NZ, 4, SLICE, TOK), bf16),
            pltpu.VMEM((NZ, 4, SLICE, TOK), bf16),
            pltpu.VMEM((NZ, 4, SLICE, TOK), bf16),
            pltpu.VMEM((NZ, 4, SLICE, TOK), bf16),
            pltpu.VMEM((NZ, SLICE, TOK), bf16),
            pltpu.VMEM((NZ, SLICE, TOK), bf16),
            pltpu.VMEM((FEAT, HID), f32),
            dma((4,)),
            dma((N_SENDS,)),
            dma((2 * NZ * PARTS,)),
            dma((NZ - 1,)),
            dma((8 * (NZ - 1),)),
            dma((NZ,)),
            dma((NZ,)),
            dma((8 * NZ,)),
            dma((8 * NZ,)),
            dma((NZ,)),
        ],
        compiler_params=pltpu.CompilerParams(
            collective_id=0, has_side_effects=True, vmem_limit_bytes=60 * 2**20
        ),
    )(grad_act, pre_act, inputs, weight)
    return git.T, gw


def solution(mesh):
    return jax.shard_map(
        shards,
        mesh=mesh,
        in_specs=(
            P("gz", ("gy", "gx")),
            P("gz", ("gy", "gx")),
            P("gz", "gx"),
            P("gx", ("gy", "gz")),
        ),
        out_specs=(P("gz", ("gx", "gy")), P("gx", ("gy", "gz"))),
        check_vma=False,
    )
```
